32 devices in a mesh: row: 8 (over y, x, core), col: 4 (over z).
Axes of the slice: x: 2, y: 2, z: 4, core: 2. Of those that a mesh axis runs over, the one named last changes fastest.
Arguments:
- tokens: bfloat16 [8192, 2048], P('row', 'col'), may hold values from -6 to 6
- heads_weight: bfloat16 [3, 2048, 2048], P(None, 'row', 'col'), may hold values from -0.125 to 0.125
- merge_weight: bfloat16 [2048, 2048], P('row', 'col'), may hold values from -4 to 4
- expand_weight: bfloat16 [2, 2048, 8192], P(None, 'row', 'col'), may hold values from -0.125 to 0.125
- shrink_weight: bfloat16 [8192, 2048], P('row', 'col'), may hold values from -0.0625 to 0.0625
- first_gain: float32 [2048], P('col'), may hold values from 0.5 to 1.5
- second_gain: float32 [2048], P('col'), may hold values from 0.5 to 1.5
- cotangent: bfloat16 [8192, 2048], P('row', 'col'), may hold values from -10 to 10
Outputs:
- layer_output: bfloat16 [8192, 2048], P('row', 'col')
- tokens_grad: float32 [8192, 2048], P('row', 'col')
- heads_grad: float32 [3, 2048, 2048], P(None, 'row', 'col')
- merge_grad: float32 [2048, 2048], P('row', 'col')
- expand_grad: float32 [2, 2048, 8192], P(None, 'row', 'col')
- shrink_grad: float32 [8192, 2048], P('row', 'col')
- first_gain_grad: float32 [2048], P('col')
- second_gain_grad: float32 [2048], P('col')
The draws below stay inside these ranges and needn't reach their ends.
All inputs are finite; a program needn't handle non-finite values.
Results may differ from the reference program's by a relative error of at most 0.012.
The reference program's roundings to bfloat16 on the way count: a program that leaves them out, or rounds other values in their place, can miss the bound.
Values may be sent and summed in bfloat16 or wider, within the bound.
A program may use at most 256 MiB of HBM per device.

```python
import math
import jax
import jax.numpy as jnp
from jax import lax

D = 2048
HEADS = 32
HEAD_DIM = 64
FF = 8192
TOK_DEV = 1024
TOKENS = 8192
N_ROW = 8


def draw_cotangent(key, part):
    key = jax.random.fold_in(key, 7)
    first_key, second_key = jax.random.split(key)
    position = jnp.arange(TOKENS, dtype=jnp.float32) / TOKENS
    base = jnp.clip(jax.random.normal(first_key, (TOKENS, D), jnp.float32), -4.0, 4.0)
    ramp = 0.5 + position
    rowscale = jnp.exp(jax.random.uniform(second_key, (TOKENS, 1), jnp.float32, -0.5, 0.5))
    return (base * ramp[:, None] * rowscale).astype(jnp.bfloat16)


def levels(rng, shape, shards, low, high):
    factor_of, own = 1.0, jax.random.fold_in(rng, 6)
    for dim, parts in shards:
        steps = jnp.exp(jax.random.uniform(jax.random.fold_in(own, dim), (parts,), jnp.float32, low / len(shards), high / len(shards)))
        factor_of = factor_of * jnp.repeat(steps, shape[dim] // parts).reshape([-1 if axis == dim else 1 for axis in range(len(shape))])
    return factor_of


def normal_values(stream_key, shape, spread, limit, cuts=(), kind=jnp.bfloat16):
    factor_of = levels(stream_key, shape, cuts, -0.22, 0.18) if cuts else 1.0
    entries = jax.random.normal(stream_key, shape, jnp.float32) * spread * factor_of
    return jnp.minimum(jnp.maximum(entries, -limit), limit).astype(kind)


def setup_inputs(seed: int = 0) -> dict:
    streams_of = jax.random.split(jax.random.key(seed), 9)
    tokens = normal_values(streams_of[0], (TOKENS, D), 1.0, 6.0, ((0, 8), (1, 4)))
    heads_weight = normal_values(streams_of[1], (3, D, D), D ** -0.5, 0.125, ((1, 8), (2, 4)))
    merge_weight = normal_values(streams_of[2], (D, D), (max(D // TOK_DEV, 1)) ** -0.5, 4.0, ((0, 8), (1, 4)))
    expand_weight = normal_values(streams_of[3], (2, D, FF), D ** -0.5, 0.125, ((1, 8), (2, 4)))
    shrink_weight = normal_values(streams_of[4], (FF, D), FF ** -0.5, 0.0625, ((0, 8), (1, 4)))
    first_gain = jnp.clip(1.0 + 0.1 * jax.random.normal(streams_of[5], (D,), jnp.float32), 0.5, 1.5)
    second_gain = jnp.clip(1.0 + 0.1 * jax.random.normal(streams_of[6], (D,), jnp.float32), 0.5, 1.5)
    cotangent = draw_cotangent(jax.random.fold_in(streams_of[8], 71), 0)
    return dict(tokens=tokens, heads_weight=heads_weight, merge_weight=merge_weight, expand_weight=expand_weight, shrink_weight=shrink_weight, first_gain=first_gain, second_gain=second_gain, cotangent=cotangent)


EPSILON = 1e-05
ROPE_BASE = 130000.0

@jax.custom_vjp
def low(v):
    return lax.optimization_barrier(v.astype(jnp.bfloat16)).astype(jnp.float32)

@jax.custom_vjp
def low_back(v):
    return v

def low_keep(v):
    return (low(v), None)

def low_pass(kept, grad):
    return (grad,)

def back_keep(v):
    return (v, None)

def back_low(kept, grad):
    return (low(grad),)
low.defvjp(low_keep, low_pass)
low_back.defvjp(back_keep, back_low)

def matmul(left, right):
    return jnp.dot(left, right, precision=lax.Precision.HIGHEST)

def rotary_tables(length):
    position = jnp.arange(length, dtype=jnp.float32)
    inverse = jnp.power(ROPE_BASE, -jnp.arange(0, HEAD_DIM, 2, dtype=jnp.float32) / HEAD_DIM)
    angles = position[:, None] * inverse[None, :]
    angles = jnp.concatenate([angles, angles], axis=1)
    return (jnp.cos(angles), jnp.sin(angles))

def rotate(values, cosine, sine):
    half = HEAD_DIM // 2
    turned = jnp.concatenate([-values[..., half:], values[..., :half]], axis=-1)
    return values * cosine[:, None, :] + turned * sine[:, None, :]

def attend_one(triple):
    query, keyset, valueset = triple
    length = query.shape[0]
    factor = 1.0 / math.sqrt(HEAD_DIM)
    scores = jnp.einsum('qhd,khd->hqk', query, keyset, precision=lax.Precision.HIGHEST) * factor
    scores = low_back(scores)
    index = jnp.arange(length)
    causal = index[:, None] >= index[None, :]
    scores = jnp.where(causal[None], scores, -1e+30)
    peak = lax.optimization_barrier(jnp.max(scores, axis=-1, keepdims=True))
    raised = jnp.exp(scores - peak)
    chances = raised / lax.optimization_barrier(jnp.sum(raised, axis=-1, keepdims=True))
    return jnp.einsum('hqk,khd->qhd', low(chances), valueset, precision=lax.Precision.HIGHEST)

def forward(tokens, heads_weight, merge_weight, expand_weight, shrink_weight, first_gain, second_gain):
    first_inverse = lax.rsqrt(lax.optimization_barrier(jnp.mean(tokens * tokens, axis=1, keepdims=True)) + EPSILON)
    first_normed = low(tokens * first_inverse * first_gain)
    split_shape = (N_ROW, TOK_DEV, HEADS, HEAD_DIM)
    cosine, sine = rotary_tables(TOK_DEV)
    queries = low_back(matmul(first_normed, heads_weight[0]))
    keyset = low_back(matmul(first_normed, heads_weight[1]))
    valueset = low(low_back(matmul(first_normed, heads_weight[2])))
    queries = low(rotate(queries.reshape(split_shape), cosine, sine))
    keyset = low(rotate(keyset.reshape(split_shape), cosine, sine))
    valueset = valueset.reshape(split_shape)
    attended = lax.map(jax.checkpoint(attend_one), (queries, keyset, valueset))
    mixed = low(low_back(attended.reshape(TOKENS, D)))
    middle = tokens + low_back(matmul(mixed, merge_weight))
    second_inverse = lax.rsqrt(lax.optimization_barrier(jnp.mean(middle * middle, axis=1, keepdims=True)) + EPSILON)
    second_normed = low(middle * second_inverse * second_gain)
    gate = low_back(matmul(second_normed, expand_weight[0]))
    upward = low_back(matmul(second_normed, expand_weight[1]))
    hidden = low(jax.nn.silu(gate) * upward)
    return middle + low_back(matmul(hidden, shrink_weight))

def reference(tokens, heads_weight, merge_weight, expand_weight, shrink_weight, first_gain, second_gain, cotangent):
    floats = [item.astype(jnp.float32) for item in (tokens, heads_weight, merge_weight, expand_weight, shrink_weight, first_gain, second_gain)]
    layer, pullback = jax.vjp(forward, *floats)
    gradients = pullback(cotangent.astype(jnp.float32))
    return (layer.astype(jnp.bfloat16), gradients[0], gradients[1], gradients[2], gradients[3], gradients[4], gradients[5], gradients[6])
```

```python
import functools

import jax
import jax.numpy as jnp
import numpy as np
from jax import lax
from jax.experimental import pallas as pl
from jax.experimental.pallas import tpu as pltpu
from jax.sharding import PartitionSpec as P

HEAD_DIM = 64
EPSILON = 1e-05
ROPE_BASE = 130000.0
LOW = jnp.bfloat16
WIDE = jnp.float32
LANES = 128
VMEM_LIMIT = 58 * 1024 * 1024


def rotary_tables(length):
    position = np.arange(length, dtype=np.float32)
    inverse = np.power(
        np.float32(ROPE_BASE), -np.arange(0, HEAD_DIM, 2, dtype=np.float32) / np.float32(HEAD_DIM)
    )
    angles = position[:, None] * inverse[None, :]
    angles = np.concatenate([angles] * (2 * LANES // HEAD_DIM), axis=1)
    return (jnp.asarray(np.cos(angles)), jnp.asarray(np.sin(angles)))


def dot(left, right):
    return jnp.dot(left, right, preferred_element_type=WIDE)


def contract_rows(left, right):
    return lax.dot_general(left, right, (((0,), (0,)), ((), ())), preferred_element_type=WIDE)


def contract_last(left, right):
    return lax.dot_general(left, right, (((1,), (1,)), ((), ())), preferred_element_type=WIDE)


def whole_spec(shape):
    return pl.BlockSpec(shape, lambda *_: (0,) * len(shape), pipeline_mode=pl.Buffered(1))


def call(kernel, grid, in_specs, out_specs, out_shape, flops, moved, scratch=()):
    return pl.pallas_call(
        kernel,
        grid=grid,
        in_specs=in_specs,
        out_specs=out_specs,
        out_shape=out_shape,
        scratch_shapes=list(scratch),
        compiler_params=pltpu.CompilerParams(vmem_limit_bytes=VMEM_LIMIT),
        cost_estimate=pl.CostEstimate(flops=int(flops), bytes_accessed=int(moved), transcendentals=0),
    )


def first_half(shape):
    return lax.rem(lax.broadcasted_iota(jnp.int32, shape, 1), HEAD_DIM) < HEAD_DIM // 2


def turn_lanes(values, cosine, sine):
    half = HEAD_DIM // 2
    ahead = pltpu.roll(values, LANES - half, 1)
    behind = pltpu.roll(values, half, 1)
    return values * cosine + jnp.where(first_half(values.shape), -ahead, behind) * sine


def turn_lanes_back(values, cosine, sine):
    half = HEAD_DIM // 2
    spun = values * sine
    ahead = pltpu.roll(spun, LANES - half, 1)
    behind = pltpu.roll(spun, half, 1)
    return values * cosine + jnp.where(first_half(values.shape), ahead, -behind)


def inverse_root(stream):
    return lax.rsqrt(jnp.mean(stream * stream, axis=1, keepdims=True) + EPSILON)


def norm_back(stream, inverse, gain, upstream):
    weighted = gain * upstream
    inner = jnp.sum(weighted * stream, axis=1, keepdims=True)
    return inverse * weighted - inverse * inverse * inverse / stream.shape[1] * stream * inner


def probabilities(query, keys, start):
    tile = query.shape[0]
    square = contract_last(query, keys[start : start + tile])
    below = lax.broadcasted_iota(jnp.int32, square.shape, 0) >= lax.broadcasted_iota(
        jnp.int32, square.shape, 1
    )
    square = jnp.where(below, square, -1e30)
    peak = jnp.max(square, axis=1, keepdims=True)
    if start:
        left = contract_last(query, keys[:start])
        peak = jnp.maximum(peak, jnp.max(left, axis=1, keepdims=True))
        left = jnp.exp(left - peak)
    square = jnp.exp(square - peak)
    sums = jnp.sum(square, axis=1, keepdims=True)
    if start:
        sums = sums + jnp.sum(left, axis=1, keepdims=True)
    scale = 1.0 / sums
    if start:
        return [(0, start, left * scale), (start, start + tile, square * scale)]
    return [(start, start + tile, square * scale)]


def head_lanes(shape, head):
    lane = lax.broadcasted_iota(jnp.int32, shape, 1)
    return (lane >= head * HEAD_DIM) & (lane < (head + 1) * HEAD_DIM)


def pick_head(values, head):
    return jnp.where(head_lanes(values.shape, head), values, jnp.zeros_like(values))


def attend_pair(tile, q_ref, k_ref, v_ref, out_ref, lanes):
    keys, values = k_ref[:, lanes], v_ref[:, lanes]
    for start in range(0, q_ref.shape[0], tile):
        here = slice(start, start + tile)
        total = jnp.zeros((tile, LANES), WIDE)
        for head in range(LANES // HEAD_DIM):
            query = pick_head(q_ref[here, lanes] * (HEAD_DIM**-0.5), head)
            mixed = jnp.zeros((tile, LANES), WIDE)
            for a, b, chances in probabilities(query, keys, start):
                mixed = mixed + dot(chances.astype(LOW), values[a:b])
            total = jnp.where(head_lanes(total.shape, head), mixed, total)
        out_ref[here, lanes] = total.astype(LOW)


def attend_back_pair(
    tile, q_ref, k_ref, v_ref, up_ref, cos_ref, sin_ref, dq_ref, dk_ref, dv_ref, k_sum, v_sum
):
    rows = q_ref.shape[0]
    scale = HEAD_DIM**-0.5
    keys, values = k_ref[...], v_ref[...]
    k_sum[...] = jnp.zeros_like(k_sum)
    v_sum[...] = jnp.zeros_like(v_sum)
    for start in reversed(range(0, rows, tile)):
        here = slice(start, start + tile)
        q_total = jnp.zeros((tile, LANES), WIDE)
        for head in range(LANES // HEAD_DIM):
            query = pick_head(q_ref[here] * scale, head)
            upper = pick_head(up_ref[here], head)
            parts = probabilities(query, keys, start)
            slopes = [contract_last(upper, values[a:b]) for a, b, _ in parts]
            inner = sum(
                jnp.sum(chances * slope, axis=1, keepdims=True)
                for (_, _, chances), slope in zip(parts, slopes)
            )
            for (a, b, chances), slope in zip(parts, slopes):
                v_sum[a:b] += contract_rows(chances.astype(LOW), upper)
                back = (chances * (slope - inner)).astype(LOW)
                k_sum[a:b] += contract_rows(back, query)
                q_total = q_total + dot(back, pick_head(keys[a:b], head))
        q_total = q_total * scale
        dq_ref[here] = turn_lanes_back(q_total, cos_ref[here], sin_ref[here]).astype(LOW)
    for start in range(0, rows, tile):
        here = slice(start, start + tile)
        dk_ref[here] = turn_lanes_back(k_sum[here], cos_ref[here], sin_ref[here]).astype(LOW)
        dv_ref[here] = v_sum[here].astype(LOW)


class Home:
    def __init__(self, n_row, n_col):
        self.n = n = n_col
        self.share = n_row // n
        self.r, self.c = lax.axis_index("row"), lax.axis_index("col")
        owner, b = self.r // self.share, lax.rem(self.r, self.share)
        self.row_to = b * n + self.mix(owner - self.c)
        step = self.unmix(lax.rem(self.r, n))
        self.col_to = lax.rem(self.c + step, n)
        self.col_from = lax.rem(self.c - step + n, n)
        self.row_from = self.col_to * self.share + self.r // n

    def mix(self, step):
        step = lax.rem(step + self.n, self.n)
        return lax.rem(step, 2) * (self.n // 2) + step // 2

    def unmix(self, place):
        return lax.rem(place, self.n // 2) * 2 + place // (self.n // 2)

    def block(self, row):
        step = self.unmix(lax.rem(row, self.n))
        return row // self.n * self.n + lax.rem(self.c - step + self.n, self.n)


MESH = pl.DeviceIdType.MESH
ANY = pl.BlockSpec(memory_space=pl.ANY)


def send(src, dst, send_sem, recv_sem, **device):
    return pltpu.make_async_remote_copy(
        src_ref=src, dst_ref=dst, send_sem=send_sem, recv_sem=recv_sem, device_id=device,
        device_id_type=MESH,
    )


class Pairs:
    def __init__(self, axis, n):
        self.axis, self.n, self.pairs = axis, n, n // 2
        self.me = lax.axis_index(axis)
        self.pair, self.side = self.me // 2, lax.rem(self.me, 2)

    def index(self, step, other=False):
        side = 1 - self.side if other else self.side
        return lax.rem(self.pair + step + self.pairs, self.pairs) * 2 + side

    def to(self, index):
        return {self.axis: index}


class Move:
    def __init__(self, axis, to, src, dst, sems):
        self.away = to != lax.axis_index(axis)
        self.remote = send(src, dst, sems[0], sems[1], **{axis: to})
        self.local = pltpu.make_async_copy(src, dst, sems[2])

    def start(self):
        @pl.when(self.away)
        def _():
            self.remote.start()

        @pl.when(jnp.logical_not(self.away))
        def _():
            self.local.start()

    def finish(self):
        @pl.when(self.away)
        def _():
            self.remote.wait()

        @pl.when(jnp.logical_not(self.away))
        def _():
            self.local.wait()


def move_sems():
    return [pltpu.SemaphoreType.DMA(())] * 3


class PairGather(Pairs):
    def __init__(self, axis, n, own, view, sems):
        super().__init__(axis, n)
        self.own, self.view = own, view
        self.out, self.swap, self.recv, self.local = sems

    def peer(self, s):
        return send(
            self.own, self.view(self.me), self.out.at[s], self.recv.at[self.me],
            **self.to(self.index(s)),
        )

    def arrival(self, s, other):
        index = self.index(-s, other)
        return send(
            self.view(index), self.view(index), self.swap.at[s], self.recv.at[index],
            **self.to(self.index(0, True)),
        )

    def mine(self):
        return send(
            self.own, self.view(self.me), self.swap.at[0], self.recv.at[self.me],
            **self.to(self.index(0, True)),
        )

    def keep(self):
        return pltpu.make_async_copy(self.own, self.view(self.me), self.local)

    def start(self):
        for s in range(1, self.pairs):
            self.peer(s).start()
        self.mine().start()
        self.keep().start()

    def forward(self):
        for s in range(1, self.pairs):
            copy = self.arrival(s, False)
            copy.wait_recv()
            copy.start()

    def arrive(self):
        for s in range(self.pairs):
            self.arrival(s, True).wait_recv()
        self.keep().wait()

    def finish(self):
        for s in range(1, self.pairs):
            self.peer(s).wait_send()
            self.arrival(s, False).wait_send()
        self.mine().wait_send()


def gather_sems(n):
    return [pltpu.SemaphoreType.DMA((n // 2,))] * 2 + [
        pltpu.SemaphoreType.DMA((n,)),
        pltpu.SemaphoreType.DMA(()),
    ]


def tiles(shape, body):
    lead, rows, cols = shape
    step = min(max(65536 // cols, 16), rows)
    per = rows // step

    def run(i, carry):
        body((i // per, pl.ds(pl.multiple_of(lax.rem(i, per) * step, step), step)))
        return carry

    lax.fori_loop(0, lead * per, run, 0)


class PairScatter(Pairs):
    def __init__(self, axis, n, room, sems, source=None):
        super().__init__(axis, n)
        self.away, self.mine, self.swapped, self.got = room
        self.swap_out, self.swap_in, self.out, self.recv = sems[:4]
        self.source = source
        if source is not None:
            self.local = sems[4]

    def swap(self, k):
        source = self.away.at[k] if self.source is None else self.source(k * 2 + 1 - self.side)
        return send(
            source, self.swapped.at[k], self.swap_out.at[k], self.swap_in.at[k],
            **self.to(self.index(0, True)),
        )

    def keep(self, k):
        return pltpu.make_async_copy(
            self.source(k * 2 + self.side), self.mine.at[k], self.local.at[k]
        )

    def start(self):
        for k in range(self.pairs):
            self.swap(k).start()
            self.keep(k).start()

    def peer(self, s):
        index = self.index(s)
        return send(
            self.mine.at[index // 2], self.got.at[s - 1], self.out.at[s - 1], self.recv.at[s - 1],
            **self.to(index),
        )

    def put(self, index, at, value):
        k = index // 2

        @pl.when(lax.rem(index, 2) == self.side)
        def _():
            self.mine[(k,) + at] = value

        @pl.when(lax.rem(index, 2) != self.side)
        def _():
            self.away[(k,) + at] = value

    def pass_on(self, index):
        @pl.when(lax.rem(index, 2) != self.side)
        def _():
            self.swap(index // 2).start()

    def exchange(self, on=True):
        for s in list(range(1, self.pairs)) + [0]:
            k = self.index(s) // 2
            self.swap(k).wait_recv()
            if self.source is not None:
                self.keep(k).wait()

            block = self.mine.shape[1:]

            def add(here):
                at = (k,) + here[3 - len(block) :]
                self.mine[at] = self.mine[at] + self.swapped[at]

            tiles((1,) * (3 - len(block)) + block, add)
            if on and s:
                self.peer(s).start()

    def arrive(self):
        for s in range(1, self.pairs):
            self.peer(s).wait_recv()

    def total(self, here):
        total = self.mine[(self.pair,) + here].astype(WIDE)
        for s in range(1, self.pairs):
            total = total + self.got[(s - 1,) + here].astype(WIDE)
        return total

    def finish(self):
        for k in range(self.pairs):
            self.swap(k).wait_send()
        for s in range(1, self.pairs):
            self.peer(s).wait_send()


def scatter_sems(n, lead=None, source=False):
    pairs = n // 2
    lead = () if lead is None else (lead,)
    sems = [pltpu.SemaphoreType.DMA(lead + (pairs,))] * 2
    sems += [pltpu.SemaphoreType.DMA(lead + (pairs - 1,))] * 2
    return sems + ([pltpu.SemaphoreType.DMA(lead + (pairs,))] if source else [])


def scatter_room(n, block, lead=None, source=False):
    pairs = n // 2
    lead = () if lead is None else (lead,)
    room = [pltpu.VMEM(lead + (pairs,) + block, LOW)] * (2 if source else 3)
    return room + [pltpu.VMEM(lead + (pairs - 1,) + block, LOW)]


def greet(pairs=(), everyone=()):
    barrier = pltpu.get_barrier_semaphore()
    count = 0

    def hello(device):
        pl.semaphore_signal(barrier, inc=1, device_id=device, device_id_type=MESH)

    for axis, n in pairs:
        place = Pairs(axis, n)
        for s in range(1, place.pairs):
            hello(place.to(place.index(s)))
        hello(place.to(place.index(0, True)))
        count += place.pairs
    for axis, n in everyone:
        for s in range(1, n):
            hello({axis: lax.rem(lax.axis_index(axis) + s, n)})
        count += n - 1
    pl.semaphore_wait(barrier, count)


class ColScatter:
    def __init__(self, n, view, own, got, sems):
        self.n, self.view, self.own, self.got = n, view, own, got
        self.out, self.recv, self.local = sems
        self.c = lax.axis_index("col")

    def copy(self, s):
        to = lax.rem(self.c + s, self.n)
        return send(
            self.view(to), self.got.at[s - 1], self.out.at[s - 1], self.recv.at[s - 1], col=to
        )

    def keep(self):
        return pltpu.make_async_copy(self.view(self.c), self.own, self.local)

    def start(self):
        for s in range(1, self.n):
            self.copy(s).start()
        self.keep().start()

    def arrive(self):
        self.keep().wait()
        for s in range(1, self.n):
            self.copy(s).wait_recv()

    def total(self, here):
        total = self.own[here].astype(WIDE)
        for s in range(1, self.n):
            total = total + self.got[(s - 1,) + here].astype(WIDE)
        return total

    def finish(self):
        for s in range(1, self.n):
            self.copy(s).wait_send()


def col_sems(n):
    return [pltpu.SemaphoreType.DMA((n - 1,))] * 2 + [pltpu.SemaphoreType.DMA(())]


def columns(ref, width):
    lead = (slice(None),) * (len(ref.shape) - 1)
    return lambda j: ref.at[lead + (pl.ds(pl.multiple_of(j * width, width), width),)]


def row_blocks(ref, depth):
    return lambda r: ref.at[:, pl.ds(pl.multiple_of(r * depth, depth), depth), :]


def talk(
    kernel, ident, in_specs, out_specs, out_shape, scratch, flops=0, moved=1 << 24, grid=()
):
    return pl.pallas_call(
        kernel,
        grid=grid,
        in_specs=in_specs,
        out_specs=out_specs,
        out_shape=out_shape,
        scratch_shapes=scratch,
        compiler_params=pltpu.CompilerParams(
            vmem_limit_bytes=VMEM_LIMIT, collective_id=ident, has_side_effects=True
        ),
        cost_estimate=pl.CostEstimate(flops=int(flops), bytes_accessed=int(moved), transcendentals=0),
    )


def gather_kernel(n_row, n_col, tokens, gains, heads, merge, shrink, *refs):
    x, gains_full, heads_full, moved, merge_rows, passing = refs[:6]
    sems = list(refs[6:])

    def take(count):
        taken, sems[:] = sems[:count], sems[count:]
        return taken

    width = tokens.shape[1]
    gain_col = PairGather("col", n_col, gains, columns(gains_full, width), take(4))
    merge_col = PairGather("col", n_col, merge, columns(merge_rows, width), take(4))
    x_col = PairGather("col", n_col, tokens, columns(x, width), take(4))
    heads_row = PairGather("row", n_row, heads, row_blocks(heads_full, heads.shape[1]), take(4))
    home = Home(n_row, n_col)
    first_move = Move("row", home.row_to, shrink, passing, take(3))
    second_move = Move("col", home.col_to, passing, moved, take(3))

    greet((), (("row", n_row), ("col", n_col)))
    gain_col.start()
    merge_col.start()
    first_move.start()
    heads_row.start()
    x_col.start()
    gain_col.forward()
    merge_col.forward()
    first_move.finish()
    second_move.start()
    heads_row.forward()
    x_col.forward()
    for job in (heads_row, gain_col, merge_col, x_col):
        job.arrive()
    for job in (heads_row, gain_col, merge_col, x_col, second_move):
        job.finish()


def gather_first(n_row, n_col, tokens, gains, heads, merge, shrink):
    rows, width = tokens.shape
    lead, depth, cols = heads.shape
    merge = merge.reshape((1,) + merge.shape)
    shape = jax.ShapeDtypeStruct
    return talk(
        functools.partial(gather_kernel, n_row, n_col),
        0,
        [ANY] * 5,
        [ANY] * 5,
        [
            shape((rows, width * n_col), LOW),
            shape((gains.shape[0], width * n_col), WIDE),
            shape((lead, depth * n_row, cols), LOW),
            shape(shrink.shape, LOW),
            shape((1, merge.shape[1], width * n_col), LOW),
        ],
        [pltpu.VMEM(shrink.shape, LOW)] + gather_sems(n_col) * 3 + gather_sems(n_row) + move_sems() * 2,
    )(tokens, gains, heads, merge, shrink)


def attend_all_kernel(
    n_row, n_col, steps, x_ref, gain_ref, w_ref, cos_ref, sin_ref, cot, moved, merge_rows,
    normed_ref, q_ref, k_ref, v_ref, cot_full, mixed, spread, merge_full, attended, *sems,
):
    step = pl.program_id(0)
    tile, width = x_ref.shape[0], attended.shape[1]
    half = cot_full.shape[0]
    cot_col = PairGather(
        "col", n_col, cot.at[pl.ds(0, half)], columns(cot_full, width), sems[:4]
    )
    mixed_col = PairGather("col", n_col, attended, columns(mixed, width), sems[4:8])
    home = Home(n_row, n_col)
    shrink_row = PairGather("row", n_row, moved, lambda r: spread.at[home.block(r)], sems[8:12])
    merge_row = PairGather(
        "row", n_row, merge_rows, row_blocks(merge_full, merge_rows.shape[1]), sems[12:16]
    )

    @pl.when(step == 0)
    def _():
        greet((("row", n_row), ("col", n_col)))
        cot_col.start()
        merge_row.start()
        shrink_row.start()

    @pl.when(step < steps)
    def _():
        rows = pl.ds(pl.multiple_of(step * tile, tile), tile)
        stream = x_ref[...].astype(WIDE)
        normed = (stream * inverse_root(stream) * gain_ref[...]).astype(LOW)
        normed_ref[...] = normed
        cosine, sine = cos_ref[rows], sin_ref[rows]
        for p, out in enumerate((q_ref, k_ref, v_ref)):
            projected = dot(normed, w_ref[p])
            for i in range(width // LANES):
                part = projected[:, i * LANES : (i + 1) * LANES]
                if p < 2:
                    part = turn_lanes(part, cosine, sine)
                out[rows, i * LANES : (i + 1) * LANES] = part.astype(LOW)

    @pl.when(step >= steps)
    def _():
        lanes = pl.ds(pl.multiple_of(jnp.maximum(step - steps, 0) * LANES, LANES), LANES)
        attend_pair(tile, q_ref, k_ref, v_ref, attended, lanes)

    @pl.when(step == steps + width // LANES // 2 - 1)
    def _():
        cot_col.forward()

    @pl.when(step == steps + width // LANES - 1)
    def _():
        mixed_col.start()
        merge_row.forward()
        shrink_row.forward()
        mixed_col.forward()
        for job in (merge_row, shrink_row, cot_col, mixed_col):
            job.arrive()
        for job in (merge_row, shrink_row, cot_col, mixed_col):
            job.finish()


def attend_all(n_row, n_col, x, gain, weight, cosine, sine, cot, moved, merge_rows):
    rows, full = x.shape
    width = full // n_col
    tile = min(256, rows)
    steps = rows // tile
    shape = jax.ShapeDtypeStruct
    low = lambda *dims: shape(dims, LOW)
    row = pl.BlockSpec((tile, full), lambda i: (jnp.minimum(i, steps - 1), 0))
    head = whole_spec((rows, width))
    return talk(
        functools.partial(attend_all_kernel, n_row, n_col, steps),
        1,
        [row, whole_spec((1, full)), whole_spec(weight.shape)]
        + [whole_spec((rows, LANES))] * 2
        + [ANY] * 3,
        [row, head, head, head] + [ANY] * 4,
        [low(rows, full)]
        + [low(rows, width)] * 3
        + [low(rows // 2, full), low(rows, full)]
        + [low(n_row, *moved.shape), low(1, merge_rows.shape[1] * n_row, full)],
        [pltpu.VMEM((rows, width), LOW)] + gather_sems(n_col) * 2 + gather_sems(n_row) * 2,
        grid=(steps + width // LANES,),
    )(x, gain, weight, cosine, sine, cot, moved, merge_rows)


def feed_kernel(
    n_row, n_col, steps, x_ref, mixed_ref, merge_ref, gain_ref, w_ref, s_ref, up_ref, cot,
    middle_ref, normed_ref, hidden_ref, gate_ref, upward_ref, grad_ref,
    later, early, *sems,
):
    step = pl.program_id(0)
    tile, full = x_ref.shape
    half = up_ref.shape[0]
    cols = s_ref.shape[3]
    units = hidden_ref.shape[1]
    each = (pl.num_programs(0) - steps) // 2
    cot_col = PairGather(
        "col", n_col, cot.at[pl.ds(half, half)], columns(later, full // n_col), sems
    )
    home = Home(n_row, n_col)

    @pl.when(step == 0)
    def _():
        greet((("col", n_col),))
        cot_col.start()

    @pl.when(step < steps)
    def _():
        rows = pl.ds(pl.multiple_of(jnp.minimum(step, steps - 1) * tile, tile), tile)
        chunk = min(512, full)
        for at in range(0, full, chunk):
            here = slice(at, at + chunk)
            middle_ref[:, here] = x_ref[:, here].astype(WIDE) + dot(
                mixed_ref[...], merge_ref[:, here]
            )

        def norm(i, carry):
            here = pl.ds(pl.multiple_of(i * 32, 32), 32)
            to = pl.ds(pl.multiple_of(jnp.minimum(step, steps - 1) * tile + i * 32, 32), 32)
            middle = middle_ref[here]
            normed_ref[to] = (middle * inverse_root(middle) * gain_ref[...]).astype(LOW)
            return carry

        lax.fori_loop(0, tile // 32, norm, 0)

    @pl.when(step == steps + each // 2)
    def _():
        cot_col.forward()

    @pl.when(step == steps + each)
    def _():
        cot_col.arrive()

    def run(first, upstream):
        block = half
        for start in range(0, half, block):
            here = slice(start, start + block)
            normed = normed_ref[first + start : first + start + block]
            gate = dot(normed, w_ref[0])
            upward = dot(normed, w_ref[1])
            back = sum(
                contract_last(upstream[here, j * cols : (j + 1) * cols], s_ref[0, j])
                for j in range(n_col)
            )
            chance = 1.0 / (1.0 + jnp.exp(-gate))
            active = gate * chance
            hidden_ref[here] = (active * upward).astype(LOW)
            gate_ref[here] = (back * upward * chance * (1.0 + gate * (1.0 - chance))).astype(LOW)
            upward_ref[here] = (back * active).astype(LOW)

    @pl.when((step >= steps) & (step < steps + each))
    def _():
        run(0, up_ref)
        early[jnp.clip(step - steps, 0, each - 1)] = hidden_ref[...]

    @pl.when(step >= steps + each)
    def _():
        run(half, later)
        turned = hidden_ref[...].T
        before = early[jnp.clip(step - steps - each, 0, each - 1)].T
        for j in range(n_col):
            here = slice(j * cols, (j + 1) * cols)
            grad_ref[home.mix(home.c - j)] = (
                dot(before, up_ref[:, here]) + dot(turned, later[:, here])
            ).astype(LOW)

    @pl.when(step == pl.num_programs(0) - 1)
    def _():
        cot_col.finish()


def feed_forward(n_row, n_col, x, mixed, merge, gain, expand, shrink, upstream, cotangent):
    rows, full = x.shape
    units = expand.shape[2]
    share, _, depth, cols = shrink.shape
    half = rows // 2
    tile = min(512, rows)
    steps = rows // tile
    part = min(256, depth)
    each, per = units // part, depth // part
    shape = jax.ShapeDtypeStruct
    row = pl.BlockSpec((tile, full), lambda i: (jnp.minimum(i, steps - 1), 0))
    past = lambda i: jnp.maximum(i - steps, 0)
    unit = lambda i: lax.rem(past(i), each)
    late = lambda i: jnp.maximum(past(i) - each, 0)
    out = pl.BlockSpec((half, part), lambda i: (past(i) // each, unit(i)))
    return talk(
        functools.partial(feed_kernel, n_row, n_col, steps),
        5,
        [
            row,
            row,
            whole_spec(merge.shape),
            whole_spec((1, full)),
            pl.BlockSpec((2, full, part), lambda i: (0, 0, unit(i))),
            pl.BlockSpec((1, n_col, part, cols), lambda i: (unit(i) // per, 0, lax.rem(unit(i), per), 0)),
            whole_spec((half, full)),
            ANY,
        ],
        [
            row,
            whole_spec((rows, full)),
            out,
            out,
            out,
            pl.BlockSpec((n_col, part, cols), lambda i: (late(i) // per, lax.rem(late(i), per), 0)),
        ],
        [shape((rows, full), WIDE), shape((rows, full), LOW)]
        + [shape((rows, units), LOW)] * 3
        + [shape((share * n_col, depth, cols), LOW)],
        [pltpu.VMEM((half, full), LOW), pltpu.VMEM((each, half, part), LOW)] + gather_sems(n_col),
        grid=(steps + 2 * each,),
    )(x, mixed, merge, gain, expand, shrink, upstream, cotangent)


def second_kernel(
    n_row, n_col, steps, gate_ref, upward_ref, w_ref, middle_ref, gain_ref, cot_ref,
    merge_ref, normed_ref, part_ref, grad_ref, out_ref, sum_ref,
    up, away, mine, swapped, got, turned, *sems,
):
    step = pl.program_id(0)
    c = lax.axis_index("col")
    tile, width = cot_ref.shape

    jobs = [
        PairScatter(
            "col", n_col, [ref.at[a] for ref in (away, mine, swapped, got)], [ref.at[a] for ref in sems]
        )
        for a in range(steps)
    ]

    @pl.when(step == 0)
    def _():
        greet((("col", n_col),))
        sum_ref[...] = jnp.zeros_like(sum_ref)

    @pl.when(step < steps)
    def _():
        a = jnp.minimum(step, steps - 1)
        rows = pl.ds(pl.multiple_of(a * tile, tile), tile)
        full = middle_ref.shape[1]
        chunk = min(512, full)
        for at in range(0, full, chunk):
            cols = slice(at, at + chunk)
            up[:, cols] = contract_last(gate_ref[rows], w_ref[0, cols]) + contract_last(
                upward_ref[rows], w_ref[1, cols]
            )

        def norm(i, carry):
            here = pl.ds(pl.multiple_of(i * 32, 32), 32)
            middle, upstream = middle_ref[here], up[here]
            inverse = inverse_root(middle)
            sum_ref[...] += jnp.sum(upstream * (middle * inverse), axis=0, keepdims=True)
            result = norm_back(middle, inverse, gain_ref[...], upstream)
            cotangent = cot_ref[here].astype(WIDE)
            for j in range(n_col):
                mine = (c == j).astype(WIDE)
                part_ref[here, j * width : (j + 1) * width] = (
                    result[:, j * width : (j + 1) * width] + mine * cotangent
                ).astype(LOW)
            return carry

        lax.fori_loop(0, tile // 32, norm, 0)
        for at in range(0, full, chunk):
            cols = slice(at, at + chunk)
            up[:, cols] = contract_last(part_ref[...], merge_ref[cols])
        place = Pairs("col", n_col)
        for j in range(n_col):
            value = up[:, j * width : (j + 1) * width].astype(LOW)

            @pl.when(j % 2 == place.side)
            def _():
                mine[a, j // 2] = value

            @pl.when(j % 2 != place.side)
            def _():
                away[a, j // 2] = value

        for index, job in enumerate(jobs):

            @pl.when(step == index)
            def _():
                for j in range(n_col):
                    job.pass_on(j)

    for index, job in enumerate(jobs):

        @pl.when(step == (index + 2 if index + 2 < steps else steps + 5 * (index + 3 - steps)))
        def _():
            job.exchange()

    @pl.when(step >= steps)
    def _():
        which = lax.rem(step - steps, 2)
        units = gate_ref.shape[1]
        chunk = min(512, units)

        @pl.when(which == 0)
        def _():
            turned[...] = normed_ref[...].T

        for index, ref in enumerate((gate_ref, upward_ref)):

            @pl.when(which == index)
            def _():
                for at in range(0, units, chunk):
                    grad_ref[0, :, at : at + chunk] = dot(
                        turned[...], ref[:, at : at + chunk]
                    ).astype(LOW)

    @pl.when(step == pl.num_programs(0) - 1)
    def _():
        for a, job in enumerate(jobs):
            job.arrive()

            def add(here):
                out_ref[(a,) + here[1:]] = job.total(here[1:]).astype(LOW)

            tiles((1,) + out_ref.shape[1:], add)
        for job in jobs:
            job.finish()


def second_back(n_row, n_col, gate, upward, expand, middle, gain, cotangent, merge, normed):
    rows, full = middle.shape
    units = gate.shape[1]
    width = full // n_col
    tile = min(256, rows)
    steps = rows // tile
    depth = min(256, full)
    later = 2 * (full // depth)
    shape = jax.ShapeDtypeStruct
    row = lambda w: pl.BlockSpec((tile, w), lambda i: (jnp.minimum(i, steps - 1), 0))
    block = (steps, tile, width)
    past = lambda i: jnp.maximum(i - steps, 0)
    outs = talk(
        functools.partial(second_kernel, n_row, n_col, steps),
        2,
        [
            whole_spec((rows, units)),
            whole_spec((rows, units)),
            whole_spec(expand.shape),
            row(full),
            whole_spec((1, full)),
            row(width),
            whole_spec(merge.shape),
            pl.BlockSpec((rows, depth), lambda i: (0, past(i) // 2)),
        ],
        [
            row(full),
            pl.BlockSpec((1, depth, units), lambda i: (lax.rem(past(i), 2), past(i) // 2, 0)),
            whole_spec(block),
            whole_spec((1, full)),
        ],
        [
            shape((rows, full), LOW),
            shape((2, full, units), LOW),
            shape(block, LOW),
            shape((1, full), WIDE),
        ],
        [
            pltpu.VMEM((tile, full), WIDE),
        ]
        + scatter_room(n_col, (tile, width), steps)
        + [pltpu.VMEM((depth, rows), LOW)]
        + scatter_sems(n_col, steps),
        grid=(steps + later,),
    )(gate, upward, expand, middle, gain, cotangent, merge, normed)
    return outs[0], outs[1], outs[2].reshape(rows, width), outs[3]


def attend_back_kernel(
    n_row, n_col, halves, hidden_ref, s_ref, middle, mixed_ref, part_ref,
    q_ref, k_ref, v_ref, up_ref, cos_ref, sin_ref, shrink_sum,
    layer_out, merge_mine, dq_ref, dk_ref, dv_ref, shrink_out, returning,
    merge_away, merge_swap,
    away, mine, swapped, got, middle_own, k_sum, v_sum, middle_sem, back_out, back_in, back_here, *sems,
):
    step = pl.program_id(0)
    home = Home(n_row, n_col)
    back = Move("col", home.col_from, shrink_sum, returning, (back_out, back_in, back_here))
    c = lax.axis_index("col")
    tile, width = layer_out.shape[1:]
    first, second = halves * n_col, halves * n_col + n_row
    jobs = [
        PairScatter(
            "col", n_col, [ref.at[h] for ref in (away, mine, swapped, got)],
            [ref.at[h] for ref in sems[:4]],
        )
        for h in range(halves)
    ]
    place = jobs[0]
    merge_row = PairScatter(
        "row", n_row, (merge_away, merge_mine, merge_swap, None), sems[4:6] + (None, None)
    )

    def middle_copy(h):
        rows = pl.ds(h * tile, tile)
        cols = pl.ds(pl.multiple_of(c * width, width), width)
        return pltpu.make_async_copy(middle.at[rows, cols], middle_own.at[h], middle_sem.at[h])

    @pl.when(step == 0)
    def _():
        greet((("row", n_row),), (("col", n_col),))
        for h in range(halves):
            middle_copy(h).start()

    @pl.when(step == second - 1)
    def _():
        back.start()

    for h, job in enumerate(jobs):

        @pl.when((step >= h * n_col) & (step < (h + 1) * n_col))
        def _():
            at = jnp.clip(step - h * n_col, 0, n_col - 1)
            k = lax.rem(at, place.pairs)
            side = jnp.where(at < place.pairs, 1 - place.side, place.side)
            j = k * 2 + side
            rows = s_ref.shape[2]
            here = slice(h * tile, (h + 1) * tile)
            value = sum(
                dot(hidden_ref[here, i * rows : (i + 1) * rows], s_ref[i, j])
                for i in range(s_ref.shape[0])
            ).astype(LOW)

            @pl.when(at < place.pairs)
            def _():
                job.away[k] = value
                job.swap(k).start()

            @pl.when(at >= place.pairs)
            def _():
                job.mine[k] = value

    @pl.when((step >= first) & (step < second))
    def _():
        row = jnp.clip(step - first, 0, n_row - 1)
        turned = mixed_ref[...].T
        full = part_ref.shape[1]
        chunk = min(512, full)
        for at in range(0, full, chunk):
            merge_row.put(
                row,
                (0, slice(None), slice(at, at + chunk)),
                dot(turned, part_ref[:, at : at + chunk]).astype(LOW),
            )
        merge_row.pass_on(row)

    @pl.when(step >= second)
    def _():
        attend_back_pair(
            min(256, q_ref.shape[0]), q_ref, k_ref, v_ref, up_ref, cos_ref, sin_ref,
            dq_ref, dk_ref, dv_ref, k_sum, v_sum,
        )

    @pl.when(step == second)
    def _():
        merge_row.exchange(False)

    for h, job in enumerate(jobs):

        @pl.when(step == (second - 1 if h == 0 else pl.num_programs(0) - 2))
        def _():
            job.exchange()

    @pl.when(step == pl.num_programs(0) - 1)
    def _():
        for h, job in enumerate(jobs):
            job.arrive()
            middle_copy(h).wait()

            def add(here):
                at = (h,) + here[1:]
                layer_out[at] = (middle_own[at] + job.total(here[1:])).astype(LOW)

            tiles((1, tile, width), add)
        back.finish()
        store = pltpu.make_async_copy(returning, shrink_out, back_here)
        store.start()
        for job in jobs:
            job.finish()
        for k in range(merge_row.pairs):
            merge_row.swap(k).wait_send()
        store.wait()


def attend_back(
    n_row, n_col, hidden, shrink, middle, mixed, part, queries, keys, values, upstream, cosine, sine,
    shrink_sum,
):
    rows, full = middle.shape
    width = full // n_col
    merge_depth = full // n_row
    shape = jax.ShapeDtypeStruct
    halves = 2
    last = halves * n_col + n_row
    pairs = width // LANES
    tile = rows // halves
    block = (halves, tile, width)
    merge_block = (n_row // 2, 1, merge_depth, full)
    merge_row = lambda i: jnp.clip(i - halves * n_col, 0, n_row - 1)
    pair = pl.BlockSpec((rows, LANES), lambda i: (0, jnp.maximum(i - last, 0)))
    table = whole_spec((rows, LANES))
    outs = talk(
        functools.partial(attend_back_kernel, n_row, n_col, halves),
        3,
        [
            whole_spec(hidden.shape),
            whole_spec(shrink.shape),
            ANY,
            pl.BlockSpec((rows, merge_depth), lambda i: (0, merge_row(i))),
            whole_spec(part.shape),
            pair, pair, pair, pair, table, table,
            ANY,
        ],
        [
            whole_spec(block),
            whole_spec(merge_block),
            pair, pair, pair,
            ANY,
        ],
        [shape(block, LOW), shape(merge_block, LOW)]
        + [shape((rows, width), LOW)] * 3
        + [shape(shrink_sum.shape, LOW)],
        [pltpu.VMEM(shrink_sum.shape, LOW)]
        + [pltpu.VMEM(merge_block, LOW)] * 2
        + scatter_room(n_col, (tile, width), halves)
        + [pltpu.VMEM(block, WIDE)]
        + [pltpu.VMEM((rows, LANES), WIDE)] * 2
        + [pltpu.SemaphoreType.DMA((halves,))]
        + move_sems()
        + scatter_sems(n_col, halves)
        + [pltpu.SemaphoreType.DMA((n_row // 2,))] * 2,
        grid=(last + pairs,),
    )(
        hidden, shrink, middle, mixed, part,
        queries, keys, values, upstream, cosine, sine, shrink_sum,
    )
    return outs[0].reshape(rows, width), outs[1], outs[2:5], outs[5]


def finish_kernel(
    n_row, n_col, steps, q_ref, k_ref, v_ref, w_ref, x_ref, gain_ref, part_ref, normed_ref, second_ref,
    merge, returning, tokens_out, heads_out, merge_out, gains_out, shrink_out,
    came, up, away, mine, swapped, got, heads_away, heads_mine, heads_swap, heads_got,
    merge_mine, merge_got, merge_sum, merge_own, merge_cols,
    gains, gains_own, gains_got, gains_all, gains_send, gains_recv, *sems,
):
    step = pl.program_id(0)
    last = pl.num_programs(0) - 1
    r = lax.axis_index("row")
    tile, full = x_ref.shape
    width = full // n_col
    jobs = [
        PairScatter(
            "col", n_col, [ref.at[a] for ref in (away, mine, swapped, got)],
            [ref.at[a] for ref in sems[:4]],
        )
        for a in range(steps)
    ]
    heads_row = PairScatter(
        "row", n_row, (heads_away, heads_mine, heads_swap, heads_got), sems[4:8]
    )
    merge_row = PairScatter(
        "row", n_row, (None, merge, None, merge_got), (None, None) + sems[8:10]
    )
    merge_keep = pltpu.make_async_copy(merge.at[merge_row.pair], merge_mine, sems[10])
    merge_col = ColScatter(n_col, columns(merge_sum, width), merge_own, merge_cols, sems[11:14])
    gains_col = ColScatter(n_col, columns(gains, width), gains_own, gains_got, sems[14:17])
    back = Move("row", Home(n_row, n_col).row_from, returning, came, sems[17:20])

    def spread(s):
        to = lax.rem(r + s, n_row)
        return send(gains_all.at[r], gains_all.at[r], gains_send.at[s - 1], gains_recv.at[r], row=to)

    def gained(s):
        at = lax.rem(r - s + n_row, n_row)
        return send(gains_all.at[at], gains_all.at[at], gains_send.at[s - 1], gains_recv.at[at], row=at)

    @pl.when(step == 0)
    def _():
        greet((), (("row", n_row), ("col", n_col)))
        for s in range(1, merge_row.pairs):
            merge_row.peer(s).start()
        merge_keep.start()
        back.start()
        gains[...] = second_ref[...]

    @pl.when(step < steps)
    def _():
        a = jnp.minimum(step, steps - 1)
        rows = pl.ds(pl.multiple_of(a * tile, tile), tile)
        chunk = min(512, full)
        for at in range(0, full, chunk):
            cols = slice(at, at + chunk)
            up[:, cols] = sum(
                contract_last(ref[rows], w_ref[p, cols]) for p, ref in enumerate((q_ref, k_ref, v_ref))
            )

        def norm(i, carry):
            here = pl.ds(pl.multiple_of(i * 32, 32), 32)
            stream, upstream = x_ref[here].astype(WIDE), up[here]
            inverse = inverse_root(stream)
            gains[0:1] += jnp.sum(upstream * (stream * inverse), axis=0, keepdims=True)
            result = norm_back(stream, inverse, gain_ref[...], upstream)
            up[here] = result + part_ref[here].astype(WIDE)
            return carry

        lax.fori_loop(0, tile // 32, norm, 0)
        place = Pairs("col", n_col)
        for j in range(n_col):
            value = up[:, j * width : (j + 1) * width].astype(LOW)

            @pl.when(j % 2 == place.side)
            def _():
                mine[a, j // 2] = value

            @pl.when(j % 2 != place.side)
            def _():
                away[a, j // 2] = value

        for index, job in enumerate(jobs):

            @pl.when(step == index)
            def _():
                for j in range(n_col):
                    job.pass_on(j)

    @pl.when(step == steps - 1)
    def _():
        gains_col.start()

    @pl.when(step >= steps)
    def _():
        row = jnp.maximum(step - steps, 0)
        turned = normed_ref[...].T
        for p, ref in enumerate((q_ref, k_ref, v_ref)):
            heads_row.put(row, (p,), dot(turned, ref[...]).astype(LOW))
        heads_row.pass_on(row)

    @pl.when(step == last)
    def _():
        heads_row.exchange()
        gains_col.arrive()
        gains_all[r] = gains_col.total((slice(None), slice(None)))
        for s in range(1, n_row):
            spread(s).start()

    for index, job in enumerate(jobs):

        @pl.when(step == (steps + 1 + 3 * index if index < 2 else last))
        def _():
            job.exchange()

    @pl.when(step == last)
    def _():
        merge_row.arrive()
        merge_keep.wait()

        def merge_add(here):
            total = merge_mine[here].astype(WIDE)
            for s in range(1, merge_row.pairs):
                total = total + merge_got[(s - 1,) + here].astype(WIDE)
            merge_sum[here] = total.astype(LOW)

        tiles(merge_sum.shape, merge_add)
        merge_col.start()
        heads_row.arrive()

        def heads_add(here):
            heads_out[here] = heads_row.total(here)

        tiles(heads_out.shape, heads_add)
        back.finish()
        store = pltpu.make_async_copy(came, shrink_out, sems[19])
        store.start()
        for a, job in enumerate(jobs):
            job.arrive()

            def add(here):
                tokens_out[(a,) + here[1:]] = job.total(here[1:])

            tiles((1, tile, width), add)
        for s in range(1, n_row):
            gained(s).wait_recv()
        gains_out[...] = sum(gains_all[i] for i in range(n_row))
        merge_col.arrive()

        def merge_done(here):
            merge_out[here] = merge_col.total(here)

        tiles(merge_out.shape, merge_done)
        for s in range(1, n_row):
            spread(s).wait_send()
        for s in range(1, merge_row.pairs):
            merge_row.peer(s).wait_send()
        for job in jobs + [gains_col, heads_row, merge_col]:
            job.finish()
        store.wait()


def finish(n_row, n_col, ups, weight, x, gain, part, normed, second, merge, returning):
    rows, full = x.shape
    width = full // n_col
    lead = weight.shape[0]
    depth = full // n_row
    tile = min(256, rows)
    steps = rows // tile
    shape = jax.ShapeDtypeStruct
    row = pl.BlockSpec((tile, full), lambda i: (jnp.minimum(i, steps - 1), 0))
    block = (steps, tile, width)
    heads_block = (lead, depth, width)
    merge_block, merge_out = (1, depth, full), (1, depth, width)
    gain_rows = second.shape[0]
    outs = talk(
        functools.partial(finish_kernel, n_row, n_col, steps),
        4,
        [whole_spec((rows, width))] * 3
        + [
            whole_spec(weight.shape),
            row,
            whole_spec((1, full)),
            row,
            pl.BlockSpec((rows, depth), lambda i: (0, jnp.maximum(i - steps, 0))),
            whole_spec(second.shape),
            ANY,
            ANY,
        ],
        [
            whole_spec(block),
            whole_spec(heads_block),
            whole_spec(merge_out),
            whole_spec((gain_rows, width)),
            ANY,
        ],
        [
            shape(block, WIDE),
            shape(heads_block, WIDE),
            shape(merge_out, WIDE),
            shape((gain_rows, width), WIDE),
            shape(returning.shape, LOW),
        ],
        [pltpu.VMEM(returning.shape, LOW), pltpu.VMEM((tile, full), WIDE)]
        + scatter_room(n_col, (tile, width), steps)
        + scatter_room(n_row, heads_block)
        + [
            pltpu.VMEM(merge_block, LOW),
            pltpu.VMEM((n_row // 2 - 1,) + merge_block, LOW),
            pltpu.VMEM(merge_block, LOW),
            pltpu.VMEM(merge_out, LOW),
            pltpu.VMEM((n_col - 1,) + merge_out, LOW),
            pltpu.VMEM((gain_rows, full), WIDE),
            pltpu.VMEM((gain_rows, width), WIDE),
            pltpu.VMEM((n_col - 1, gain_rows, width), WIDE),
            pltpu.VMEM((n_row, gain_rows, width), WIDE),
            pltpu.SemaphoreType.DMA((n_row - 1,)),
            pltpu.SemaphoreType.DMA((n_row,)),
        ]
        + scatter_sems(n_col, steps)
        + scatter_sems(n_row)
        + [pltpu.SemaphoreType.DMA((n_row // 2 - 1,))] * 2
        + [pltpu.SemaphoreType.DMA(())]
        + col_sems(n_col) * 2
        + move_sems(),
        grid=(steps + n_row,),
    )(*ups, weight, x, gain, part, normed, second, merge, returning)
    return outs[0].reshape(rows, width), outs[1], outs[2][0], outs[3], outs[4]


def local(
    tokens,
    heads_weight,
    merge_weight,
    expand_weight,
    shrink_weight,
    first_gain,
    second_gain,
    cotangent,
):
    n_row, n_col = lax.axis_size("row"), lax.axis_size("col")
    length = tokens.shape[0]
    share = n_row // n_col
    shrink_rows, shrink_cols = shrink_weight.shape

    gains = jnp.stack([first_gain, second_gain] + [jnp.zeros_like(first_gain)] * 6)
    x, gains, heads_full, moved, merge_rows = gather_first(
        n_row, n_col, tokens, gains, heads_weight, merge_weight, shrink_weight
    )
    expand_full = lax.all_gather(expand_weight, "row", axis=1, tiled=True)
    first_gains, second_gains = gains[:1], gains[1:2]
    cosine, sine = rotary_tables(length)
    first_normed, queries, keys, values, upstream, mixed, shrink_full, merge_full = attend_all(
        n_row, n_col, x, first_gains, heads_full, cosine, sine, cotangent, moved, merge_rows
    )
    merge_full = merge_full[0]
    shrink_full = shrink_full.reshape(share, n_col, shrink_rows, shrink_cols)
    middle, second_normed, hidden, gate_grad, upward_grad, shrink_blocks = feed_forward(
        n_row, n_col, x, mixed, merge_full, second_gains, expand_full, shrink_full, upstream, cotangent
    )
    shrink_sum = lax.psum_scatter(shrink_blocks, "row", scatter_dimension=0)
    middle_part, expand_grad, mixed_grad, second_sum = second_back(
        n_row, n_col, gate_grad, upward_grad, expand_full, middle, second_gains, cotangent,
        merge_full, second_normed,
    )
    expand_sum = lax.psum_scatter(expand_grad, "row", scatter_dimension=1, tiled=True)
    layer_output, merge_blocks, ups, shrink_sum = attend_back(
        n_row, n_col, hidden, shrink_full, middle, mixed, middle_part,
        queries, keys, values, mixed_grad, cosine, sine, shrink_sum,
    )
    second_rows = jnp.pad(second_sum, ((1, 6), (0, 0)))
    tokens_grad, heads_sum, merge_sum, gain_sums, shrink_sum = finish(
        n_row, n_col, ups, heads_full, x, first_gains, middle_part, first_normed, second_rows,
        merge_blocks, shrink_sum,
    )
    return (
        layer_output,
        tokens_grad,
        heads_sum,
        merge_sum,
        expand_sum.astype(WIDE),
        shrink_sum.astype(WIDE),
        gain_sums[0],
        gain_sums[1],
    )


def solution(mesh):
    in_specs = (
        P("row", "col"),
        P(None, "row", "col"),
        P("row", "col"),
        P(None, "row", "col"),
        P("row", "col"),
        P("col"),
        P("col"),
        P("row", "col"),
    )
    out_specs = (
        P("row", "col"),
        P("row", "col"),
        P(None, "row", "col"),
        P("row", "col"),
        P(None, "row", "col"),
        P("row", "col"),
        P("col"),
        P("col"),
    )
    return jax.shard_map(local, mesh=mesh, in_specs=in_specs, out_specs=out_specs, check_vma=False)
```
